128 devices in a mesh: cent: 32 (over y, z, core), batch: 4 (over x).
Axes of the slice: x: 4, y: 4, z: 4, core: 2. Of those that a mesh axis runs over, the one named last changes fastest.
Arguments:
- queries: bfloat16 [4096, 768], P(('batch', 'cent')), may hold values from -8 to 8
- centroids: bfloat16 [131072, 768], P('cent'), may hold values from -40 to 40
- centroid_mass: float32 [131072], P('cent'), may hold values from 0.25 to 4
Outputs:
- query_grad: float32 [4096, 768], P(('batch', 'cent'))
The draws below stay inside these ranges and needn't reach their ends.
All inputs are finite; a program needn't handle non-finite values.
Results may differ from the reference program's by a relative error of at most 0.018.
Values may be sent and summed in bfloat16 or wider, within the bound.
No kernel may reach another device: no remote copies, remote signals or barrier semaphores. Data moves between devices by JAX's collectives and lax.ppermute only.
A program may use at most 128 MiB of HBM per device.

```python
import math
import jax
import jax.numpy as jnp
from jax import lax

D = 768
KDEV = 4096
ITERS = 3
CENTROIDS = 131072
QUERIES = 4096
N_CENT = 32


def pair_row(key, index):
    inner = jax.random.fold_in(jax.random.fold_in(key, 17), index)
    key_base, key_scale, key_noise = jax.random.split(inner, 3)
    base_row = jax.random.normal(key_base, (D,), jnp.float32)
    spread = jnp.exp(jax.random.uniform(key_scale, (), jnp.float32, math.log(0.3), math.log(3.0)))
    fresh_noise = jax.random.normal(key_noise, (D,), jnp.float32)
    return (base_row, spread, fresh_noise)


def draw_centroids(key, part):
    pair_ids = jnp.arange(CENTROIDS // 2)
    base_row, spread, fresh_noise = jax.vmap(lambda index: pair_row(key, index))(pair_ids)
    even_rows = 3.0 * base_row
    odd_rows = 3.0 * fresh_noise
    rows_all = jnp.stack([even_rows, odd_rows], axis=1).reshape(CENTROIDS, D)
    return jnp.clip(rows_all, -40.0, 40.0).astype(jnp.bfloat16)


def draw_queries(key, part):
    own_key = jax.random.fold_in(key, 5)
    key_drawn = jax.random.fold_in(own_key, 0)
    drawn_rows = jax.random.normal(key_drawn, (QUERIES, D), jnp.float32) / math.sqrt(D)
    return jnp.clip(drawn_rows, -8.0, 8.0).astype(jnp.bfloat16)


def block_scale(key, shape, shards, smallest, high):
    factor_of = 1.0
    for position, parts in shards:
        heights = jax.random.uniform(jax.random.fold_in(jax.random.fold_in(key, 6), position), (parts,), jnp.float32, smallest / len(shards), high / len(shards))
        factor_of = factor_of * jnp.repeat(jnp.exp(heights), shape[position] // parts).reshape((-1,) + (1,) * (len(shape) - 1 - position))
    return factor_of


def setup_inputs(seed: int = 0) -> dict:
    keys = jax.random.split(jax.random.key(seed), 4)
    return {
        "queries": draw_queries(jax.random.fold_in(keys[3], 71), 0),
        "centroids": draw_centroids(jax.random.fold_in(keys[3], 71), 0),
        "centroid_mass": jnp.clip(jnp.exp(math.log(4.0) - 2.7725887 * jax.random.uniform(keys[2], (CENTROIDS,), jnp.float32) ** block_scale(keys[2], (CENTROIDS,), ((0, 32),), -0.2, 0.2)), 0.25, 4.0),
    }


def exp_tile_of(query_f32, cent_block, row_top):
    scores = jnp.dot(query_f32, cent_block.astype(jnp.float32).T)
    rounded = lax.optimization_barrier(jnp.exp(scores - row_top[:, None]).astype(jnp.bfloat16))
    return rounded.astype(jnp.float32)


def reference(queries, centroids, centroid_mass):
    query_f32 = queries.astype(jnp.float32)
    centroid_blocks = centroids.reshape(N_CENT, KDEV, D)
    block_masses = centroid_mass.reshape(N_CENT, KDEV)

    def first_pass(cent_block):
        scores = jnp.dot(query_f32, cent_block.astype(jnp.float32).T)
        row_top = jnp.max(scores, axis=1)
        return row_top, jnp.sum(jnp.exp(scores - row_top[:, None]), axis=1)

    block_peak_max, block_total = lax.map(first_pass, centroid_blocks)
    row_max = jnp.max(block_peak_max, axis=0)
    balance_factor = jnp.exp(block_peak_max - row_max[None, :])
    partition = jnp.sum(balance_factor * block_total, axis=0)
    row_scales = 1.0 / partition
    column_scales = block_masses
    for sweep in range(ITERS):
        def balancing_block(input_arrays, row_weighting=row_scales):
            cent_block, factor_block, mass_block, top_block = input_arrays
            tile = exp_tile_of(query_f32, cent_block, top_block)
            column = jnp.dot(row_weighting * factor_block, tile)
            col_scale = mass_block / column
            return col_scale, factor_block * jnp.dot(tile, col_scale)

        column_scales, row_pieces = lax.map(balancing_block, (centroid_blocks, balance_factor, block_masses, block_peak_max))
        row_scales = 1.0 / jnp.sum(row_pieces, axis=0)

    def grad_block(carry, input_arrays):
        cent_block, factor_block, cols_block, top_block = input_arrays
        tile = exp_tile_of(query_f32, cent_block, top_block)
        positive = lax.optimization_barrier((tile * (factor_block / partition)[:, None]).astype(jnp.bfloat16))
        negative = lax.optimization_barrier(((tile * cols_block[None, :]) * (factor_block * row_scales)[:, None]).astype(jnp.bfloat16))
        cent_f32 = cent_block.astype(jnp.float32)
        return (carry[0] + jnp.dot(positive.astype(jnp.float32), cent_f32), carry[1] + jnp.dot(negative.astype(jnp.float32), cent_f32)), None

    zeros_grad = jnp.zeros((queries.shape[0], D), jnp.float32)
    totals, unused = lax.scan(grad_block, (zeros_grad, zeros_grad), (centroid_blocks, balance_factor, column_scales, block_peak_max))
    return totals[0] - totals[1]
```

```python
import functools

import jax
import jax.numpy as jnp
from jax import lax
from jax.experimental import pallas as pl
from jax.experimental.pallas import tpu as pltpu
from jax.sharding import PartitionSpec as P

ITERS = 3
CORE = 1
ALONG_Z = (2, 4, 6)
ALONG_Y = (8, 16, 24)
F32 = jnp.float32
BF16 = jnp.bfloat16
VMEM = pl.BlockSpec(memory_space=pltpu.VMEM)
CHUNK = 512


def call_kernel(
    kernel, outs, args, name, flops, transcendentals=0, scratch=(), scoped=12, index=None, far=()
):
    moved = sum(a.size * a.dtype.itemsize for a in list(args) + list(outs) + list(far))
    args = [pltpu.with_memory_space_constraint(a, pltpu.VMEM) for a in args]
    specs = [VMEM] * len(args)
    args = [pltpu.with_memory_space_constraint(a, pltpu.HBM) for a in far] + args
    specs = [pl.BlockSpec(memory_space=pltpu.HBM)] * len(far) + specs
    if index is not None:
        args, specs = [index] + args, [pl.BlockSpec(memory_space=pltpu.SMEM)] + specs
    return pl.pallas_call(
        kernel,
        out_shape=tuple(pltpu.VMEM(o.shape, o.dtype) for o in outs),
        in_specs=specs,
        out_specs=(VMEM,) * len(outs),
        scratch_shapes=list(scratch),
        compiler_params=pltpu.CompilerParams(vmem_limit_bytes=scoped * 2**20),
        cost_estimate=pl.CostEstimate(
            flops=flops, bytes_accessed=moved, transcendentals=transcendentals
        ),
        name=name,
    )(*args)


def lane_groups(value, op, start):
    for group in range(value.shape[1] // 128):
        part = value[:, group * 128 : (group + 1) * 128]
        start = part if start is None else op(start, part)
    return start


def to_lanes(value, op):
    return op(jnp.transpose(value), axis=0, keepdims=True)


def z_starts(index_ref):
    z = (index_ref[0] >> 1) & 3
    return [pl.multiple_of((z ^ k) * 32, 32) for k in range(4)]


def order_rows(index_ref, rows_ref, ordered):
    for m in range(rows_ref.shape[0] // 128):
        for k, start in enumerate(z_starts(index_ref)):
            rows = rows_ref[m * 128 + k * 32 : m * 128 + (k + 1) * 32, :]
            ordered[pl.ds(pl.multiple_of(m * 128 + start, 32), 32), :] = rows


def score_chunk(rows, cent_ref, score_ref, chunk, top):
    columns = slice(chunk * CHUNK, (chunk + 1) * CHUNK)
    scores = lax.dot_general(
        rows, cent_ref[columns, :], (((1,), (1,)), ((), ())), preferred_element_type=F32
    )
    score_ref[:, columns] = scores
    return lane_groups(scores, jnp.maximum, top)


def block_starts(index_ref, part):
    core, y = index_ref[0] & 1, index_ref[0] >> 3
    return [pl.multiple_of((core ^ part) * 512 + (y ^ m) * 128, 128) for m in range(4)]


def exp_chunk(score_ref, tile_ref, starts, chunk, top, total):
    columns = slice(chunk * CHUNK, (chunk + 1) * CHUNK)
    shifted = jnp.exp(score_ref[:, columns] - top)
    rounded = shifted.astype(BF16)
    for m, start in enumerate(starts):
        tile_ref[pl.ds(start, 128), columns] = rounded[m * 128 : (m + 1) * 128]
    return lane_groups(shifted, jnp.add, total)


def store_stat(out_ref, starts, lanes):
    for m, start in enumerate(starts):
        out_ref[:, pl.ds(start, 128)] = lanes[:, m * 128 : (m + 1) * 128]


def load_kernel(index_ref, far_ref, rows_ref, near_ref, out_ref, arrived):
    copy = pltpu.make_async_copy(far_ref, near_ref, arrived)
    copy.start()
    out_ref[...] = rows_ref[...]
    copy.wait()


def load_near(index, centroids, rows):
    shape = jax.ShapeDtypeStruct
    return call_kernel(
        load_kernel,
        (shape(centroids.shape, centroids.dtype), shape(rows.shape, rows.dtype)),
        (rows,),
        "load_centroids",
        0,
        scratch=[pltpu.SemaphoreType.DMA(())],
        index=index,
        far=(centroids,),
    )


def first_score_kernel(index_ref, rows_ref, cent_ref, score_ref, top_ref, ordered):
    order_rows(index_ref, rows_ref, ordered)
    rows, top = ordered[...], None
    for chunk in range(cent_ref.shape[0] // CHUNK):
        top = score_chunk(rows, cent_ref, score_ref, chunk, top)
    top_ref[...] = top


def second_score_kernel(
    index_ref, score_ref, lane_top_ref, rows_ref, cent_ref, tile_ref, top_ref, total_ref, held, ordered
):
    first, second = block_starts(index_ref, 0), block_starts(index_ref, 1)
    row_top = jnp.max(lane_top_ref[...], axis=1, keepdims=True)
    order_rows(index_ref, rows_ref, ordered)
    rows, top, total = ordered[...], None, None
    for chunk in range(cent_ref.shape[0] // CHUNK):
        top = score_chunk(rows, cent_ref, held, chunk, top)
        total = exp_chunk(score_ref, tile_ref, first, chunk, row_top, total)
    store_stat(top_ref, first, to_lanes(lane_top_ref[...], jnp.max))
    store_stat(total_ref, first, to_lanes(total, jnp.sum))
    row_top = jnp.max(top, axis=1, keepdims=True)
    total = None
    for chunk in range(cent_ref.shape[0] // CHUNK):
        total = exp_chunk(held, tile_ref, second, chunk, row_top, total)
    store_stat(top_ref, second, to_lanes(top, jnp.max))
    store_stat(total_ref, second, to_lanes(total, jnp.sum))


def score_both(index, first_rows, second_rows, near):
    rows, features = first_rows.shape
    columns = near.shape[0]
    shape = jax.ShapeDtypeStruct
    flops = 2 * rows * columns * features
    scores, lane_top = call_kernel(
        first_score_kernel,
        (shape((rows, columns), F32), shape((rows, 128), F32)),
        (first_rows, near),
        "score_first",
        flops,
        scratch=[pltpu.VMEM(first_rows.shape, BF16)],
        index=index,
    )
    stats = shape((1, 2 * rows), F32)
    tile, top, total = call_kernel(
        second_score_kernel,
        (shape((2 * rows, columns), BF16), stats, stats),
        (scores, lane_top, second_rows, near),
        "score_second",
        flops,
        2 * rows * columns,
        [pltpu.VMEM((rows, columns), F32), pltpu.VMEM(first_rows.shape, BF16)],
        scoped=20,
        index=index,
    )
    return tile, top[0], total[0]


def down_rows(vector):
    groups = [
        jnp.transpose(jnp.broadcast_to(vector[:, g * 128 : (g + 1) * 128], (128, 128)))
        for g in range(vector.shape[1] // 128)
    ]
    return jnp.concatenate(groups, axis=0)


def half_rows(index_ref, part, half):
    return pl.ds(pl.multiple_of(((index_ref[0] & 1) ^ part) * half, half), half)


def positive_kernel(part, index_ref, tile_ref, cent_ref, pass_ref, out_ref, passed_ref):
    passed_ref[...] = pass_ref[...]
    rows = half_rows(index_ref, part, out_ref.shape[0])
    out_ref[...] = jnp.dot(tile_ref[rows, :], cent_ref[...], preferred_element_type=F32)


def negative_kernel(
    part, index_ref, tile_ref, cent_ref, pass_ref, column_ref, out_ref, passed_ref
):
    passed_ref[...] = pass_ref[...]
    rows = half_rows(index_ref, part, out_ref.shape[0])
    width = 256
    total = None
    for chunk in range(tile_ref.shape[1] // width):
        columns = slice(chunk * width, (chunk + 1) * width)
        weights = (tile_ref[rows, columns].astype(F32) * column_ref[:, columns]).astype(BF16)
        product = jnp.dot(weights, cent_ref[columns, :], preferred_element_type=F32)
        total = product if total is None else total + product
    out_ref[...] = total


def half_products(kernel, index, tile, centroids, passed, *vectors):
    rows, columns = tile.shape[0] // 2, tile.shape[1]
    features = centroids.shape[1]
    shape = jax.ShapeDtypeStruct
    products, passed = [], passed[None, :]
    for part in range(2):
        product, passed = call_kernel(
            functools.partial(kernel, part),
            (shape((rows, features), F32), shape(passed.shape, passed.dtype)),
            (tile, centroids, passed) + vectors,
            kernel.__name__,
            2 * rows * columns * features,
            index=index,
        )
        products.append(product)
    return products, passed[0]


def combine_kernel(part, index_ref, positive_ref, negative_ref, up_ref, down_ref, out_ref):
    y = index_ref[0] >> 3
    repeat = positive_ref.shape[1] // 128
    for m, start in enumerate(block_starts(index_ref, part)):
        up, down = [
            jnp.concatenate([down_rows(ref[:, pl.ds(start, 128)])] * repeat, axis=1)
            for ref in (up_ref, down_ref)
        ]
        source = pl.ds(pl.multiple_of((y ^ m) * 128, 128), 128)
        rows = positive_ref[source, :] * up - negative_ref[source, :] * down
        for k, place in enumerate(z_starts(index_ref)):
            target = pl.ds(pl.multiple_of(m * 128 + place, 32), 32)
            out_ref[target, :] = rows[k * 32 : (k + 1) * 32].astype(out_ref.dtype)


def combine(part, index, positive, negative, up, down, dtype):
    return call_kernel(
        functools.partial(combine_kernel, part),
        (jax.ShapeDtypeStruct(positive.shape, dtype),),
        (positive, negative, up[None, :], down[None, :]),
        "combine",
        3 * positive.size,
        index=index,
    )[0]


def swap(value, mask):
    size = lax.axis_size("cent")
    return lax.ppermute(value, "cent", [(i, i ^ mask) for i in range(size)])


def swap_three(values, masks):
    near, far, other = masks
    first, last = swap(values[0], near), swap(values[2], other)
    return [first, swap(values[1], far), last]


def sum_cent(value):
    value = value + swap(value, CORE)
    for masks in (ALONG_Y, ALONG_Z):
        value = value + sum(swap_three([value] * 3, masks))
    return value


def sum_batch(value):
    others = [
        lax.ppermute(value, "batch", [(i, i ^ mask) for i in range(4)]) for mask in (1, 3, 2)
    ]
    return value + sum(others)


def merge_softmax(top, total):
    pair = jnp.stack([top, total])
    for masks in ((CORE,), ALONG_Y, ALONG_Z):
        pairs = [pair] + (swap_three([pair] * 3, masks) if len(masks) == 3 else [swap(pair, CORE)])
        new_top = pairs[0][0]
        for other in pairs[1:]:
            new_top = jnp.maximum(new_top, other[0])
        new_total = sum([other[1] * jnp.exp(other[0] - new_top) for other in pairs])
        pair = jnp.stack([new_top, new_total])
    return pair[0], pair[1]


def scatter_stage(blocks, masks):
    arrived = swap_three([block.astype(BF16) for block in blocks[1:]], masks)
    return blocks[0] + sum([value.astype(F32) for value in arrived])


def per_device(queries, centroids, centroid_mass):
    where = lax.axis_index("cent").astype(jnp.int32).reshape(1)
    near, own_block = load_near(where, centroids, queries)
    plane = jnp.concatenate([own_block] + swap_three([queries] * 3, ALONG_Z))
    own_rows = jnp.concatenate([plane] + swap_three([plane] * 3, ALONG_Y))
    far_rows = swap(own_rows, CORE)
    tile, block_peak_max, block_total = score_both(where, own_rows, far_rows, near)
    positive, passed = half_products(positive_kernel, where, tile, near, block_peak_max)
    row_max, partition = merge_softmax(block_peak_max, block_total)
    block_peak_max = passed
    balance_factor = jnp.exp(block_peak_max - row_max)
    up = weights = balance_factor / partition
    for sweep in range(ITERS):
        column = jnp.dot(weights, tile, preferred_element_type=F32)
        column_scales = centroid_mass / sum_batch(column)
        row_local = jnp.dot(tile, column_scales, preferred_element_type=F32)
        row_sums = sum_cent(balance_factor * row_local)
        if sweep == ITERS - 1:
            small = (column_scales * 2.0**-6)[None, :]
            negative, balance_factor = half_products(
                negative_kernel, where, tile, near, balance_factor, small
            )
        weights = balance_factor / row_sums
    down = weights * 2.0**6

    far_sum = swap(combine(1, where, positive[1], negative[1], up, down, BF16), CORE)
    rows = combine(0, where, positive[0], negative[0], up, down, F32) + far_sum.astype(F32)
    plane_sum = scatter_stage(jnp.split(rows, 4), ALONG_Y)
    return scatter_stage(jnp.split(plane_sum, 4), ALONG_Z)


def solution(mesh):
    placed = (P(("batch", "cent"), None), P("cent", None), P("cent"))
    return jax.shard_map(
        per_device,
        mesh=mesh,
        in_specs=placed,
        out_specs=P(("batch", "cent"), None),
        check_vma=False,
    )
```

```python
import jax
import jax.numpy as jnp
from jax import lax
from jax.sharding import PartitionSpec as P

ITERS = 3
CORE = 1
ALONG_Z = (2, 4, 6)
ALONG_Y = (8, 16, 24)
F32 = jnp.float32
BF16 = jnp.bfloat16


def swap(value, mask):
    size = lax.axis_size("cent")
    return lax.ppermute(value, "cent", [(i, i ^ mask) for i in range(size)])


def beside(value, work):
    if work is None:
        return value, None
    return lax.optimization_barrier((value, work()))


def sum_cent(value, works=(None, None, None)):
    results = []
    for masks, work in zip(((CORE,), ALONG_Y, ALONG_Z), works):
        value = value + sum([swap(value, mask) for mask in masks])
        value, result = beside(value, work)
        results.append(result)
    return value, results[1:]


def sum_batch(value):
    others = [
        lax.ppermute(value, "batch", [(i, i ^ mask) for i in range(4)]) for mask in (1, 3, 2)
    ]
    return value + sum(others)


def merge_softmax(top, total, works):
    pair, results = jnp.stack([top, total]), []
    for masks, work in zip(((CORE,), ALONG_Y, ALONG_Z), works):
        pairs = [pair] + [swap(pair, mask) for mask in masks]
        new_top = pairs[0][0]
        for other in pairs[1:]:
            new_top = jnp.maximum(new_top, other[0])
        new_total = sum([other[1] * jnp.exp(other[0] - new_top) for other in pairs])
        pair, result = beside(jnp.stack([new_top, new_total]), work)
        results.append(result)
    return pair[0], pair[1], results[1:]


def places(index):
    own = index.astype(jnp.uint32)
    z, y, core = (own >> 1) & 3, own >> 3, own & 1
    return [[z ^ k for k in range(4)], [y ^ k for k in range(4)], [core ^ k for k in range(2)]]


def gather_rows(queries, blocks):
    held, zero = queries, jnp.uint32(0)
    for masks, order in zip((ALONG_Z, ALONG_Y, (CORE,)), blocks):
        buffer = jnp.zeros((len(order),) + held.shape, held.dtype)
        for place, block in zip(order, [held] + [swap(held, mask) for mask in masks]):
            buffer = lax.dynamic_update_slice(buffer, block[None], (place, zero, zero))
        held = buffer.reshape((len(order) * held.shape[0],) + held.shape[1:])
    return held


def scatter_stage(partial, masks, order):
    blocks = partial.reshape(4, partial.shape[0] // 4, partial.shape[1])
    zero = jnp.uint32(0)
    mine = [
        lax.dynamic_slice(blocks, (place, zero, zero), (1,) + blocks.shape[1:])[0]
        for place in order
    ]
    arrived = [swap(block.astype(BF16), mask) for block, mask in zip(mine[1:], masks)]
    return mine[0] + sum([value.astype(F32) for value in arrived])


def half_products(weights_of, tile, centroids):
    half = tile.shape[0] // 2

    def product(start):
        rows = weights_of(tile[start : start + half])
        return jnp.dot(rows, centroids, preferred_element_type=F32)

    return None, lambda: product(0), lambda: product(half)


def per_device(queries, centroids, centroid_mass):
    index = lax.axis_index("cent")
    blocks = places(index)
    queries, blocks, second = lax.optimization_barrier((queries, blocks, blocks[2][0] == 1))
    rows = gather_rows(queries, blocks)
    scores = lax.dot_general(
        rows, centroids, (((1,), (1,)), ((), ())), preferred_element_type=F32
    )
    block_peak_max = jnp.max(scores, axis=1)
    shifted = jnp.exp(scores - block_peak_max[:, None])
    tile = shifted.astype(BF16)
    block_total = jnp.sum(shifted, axis=1)

    works = half_products(lambda rows: rows, tile, centroids)
    row_max, partition, positive = merge_softmax(block_peak_max, block_total, works)
    balance_factor = jnp.exp(block_peak_max - row_max)
    up = weights = balance_factor / partition
    for sweep in range(ITERS):
        column = jnp.dot(weights, tile, preferred_element_type=F32)
        column_scales = centroid_mass / sum_batch(column)
        row_local = jnp.dot(tile, column_scales, preferred_element_type=F32)
        works = (None,) * 3
        if sweep == ITERS - 1:
            small = (column_scales * 2.0**-6)[None, :]
            works = half_products(
                lambda rows: (rows.astype(F32) * small).astype(BF16), tile, centroids
            )
        row_sums, negative = sum_cent(balance_factor * row_local, works)
        weights = balance_factor / row_sums
    down = weights * 2.0**6

    half = tile.shape[0] // 2
    ups, downs = up.reshape(2, half, 1), down.reshape(2, half, 1)
    gradient = [positive[part] * ups[part] - negative[part] * downs[part] for part in range(2)]
    far_sum = swap(jnp.where(second, gradient[0], gradient[1]).astype(BF16), CORE)
    rows = jnp.where(second, gradient[1], gradient[0]) + far_sum.astype(F32)
    plane_sum = scatter_stage(rows, ALONG_Y, blocks[1])
    return scatter_stage(plane_sum, ALONG_Z, blocks[0])


def solution(mesh):
    placed = (P(("batch", "cent"), None), P("cent", None), P("cent"))
    return jax.shard_map(
        per_device,
        mesh=mesh,
        in_specs=placed,
        out_specs=P(("batch", "cent"), None),
        check_vma=False,
    )
```

```python
import functools

import jax
import jax.numpy as jnp
from jax import lax
from jax.experimental import pallas as pl
from jax.experimental.pallas import tpu as pltpu
from jax.sharding import PartitionSpec as P

ITERS = 3
CORE = 1
ALONG_Z = (2, 4, 6)
ALONG_Y = (8, 16, 24)
F32 = jnp.float32
BF16 = jnp.bfloat16
VMEM = pl.BlockSpec(memory_space=pltpu.VMEM)
CHUNK = 512


def call_kernel(
    kernel, outs, args, name, flops, transcendentals=0, scratch=(), scoped=12, index=None, far=()
):
    moved = sum(a.size * a.dtype.itemsize for a in list(args) + list(outs) + list(far))
    args = [pltpu.with_memory_space_constraint(a, pltpu.VMEM) for a in args]
    specs = [VMEM] * len(args)
    args = [pltpu.with_memory_space_constraint(a, pltpu.HBM) for a in far] + args
    specs = [pl.BlockSpec(memory_space=pltpu.HBM)] * len(far) + specs
    if index is not None:
        args, specs = [index] + args, [pl.BlockSpec(memory_space=pltpu.SMEM)] + specs
    return pl.pallas_call(
        kernel,
        out_shape=tuple(pltpu.VMEM(o.shape, o.dtype) for o in outs),
        in_specs=specs,
        out_specs=(VMEM,) * len(outs),
        scratch_shapes=list(scratch),
        compiler_params=pltpu.CompilerParams(vmem_limit_bytes=scoped * 2**20),
        cost_estimate=pl.CostEstimate(
            flops=flops, bytes_accessed=moved, transcendentals=transcendentals
        ),
        name=name,
    )(*args)


def lane_groups(value, op, start):
    for group in range(value.shape[1] // 128):
        part = value[:, group * 128 : (group + 1) * 128]
        start = part if start is None else op(start, part)
    return start


def to_lanes(value, op):
    return op(jnp.transpose(value), axis=0, keepdims=True)


def z_starts(index_ref):
    z = (index_ref[0] >> 1) & 3
    return [pl.multiple_of((z ^ k) * 32, 32) for k in range(4)]


def order_rows(index_ref, rows_ref, ordered):
    for m in range(rows_ref.shape[0] // 128):
        for k, start in enumerate(z_starts(index_ref)):
            rows = rows_ref[m * 128 + k * 32 : m * 128 + (k + 1) * 32, :]
            ordered[pl.ds(pl.multiple_of(m * 128 + start, 32), 32), :] = rows


def score_chunk(rows, cent_ref, score_ref, chunk, top):
    columns = slice(chunk * CHUNK, (chunk + 1) * CHUNK)
    scores = lax.dot_general(
        rows, cent_ref[columns, :], (((1,), (1,)), ((), ())), preferred_element_type=F32
    )
    score_ref[:, columns] = scores
    return lane_groups(scores, jnp.maximum, top)


def block_starts(index_ref, part):
    core, y = index_ref[0] & 1, index_ref[0] >> 3
    return [pl.multiple_of((core ^ part) * 512 + (y ^ m) * 128, 128) for m in range(4)]


def exp_chunk(score_ref, tile_ref, starts, chunk, top, total):
    columns = slice(chunk * CHUNK, (chunk + 1) * CHUNK)
    shifted = jnp.exp(score_ref[:, columns] - top)
    rounded = shifted.astype(BF16)
    for m, start in enumerate(starts):
        tile_ref[pl.ds(start, 128), columns] = rounded[m * 128 : (m + 1) * 128]
    return lane_groups(shifted, jnp.add, total)


def store_stat(out_ref, starts, lanes):
    for m, start in enumerate(starts):
        out_ref[:, pl.ds(start, 128)] = lanes[:, m * 128 : (m + 1) * 128]


def load_kernel(index_ref, far_ref, rows_ref, near_ref, out_ref, arrived):
    copy = pltpu.make_async_copy(far_ref, near_ref, arrived)
    copy.start()
    out_ref[...] = rows_ref[...]
    copy.wait()


def load_near(index, centroids, rows):
    shape = jax.ShapeDtypeStruct
    return call_kernel(
        load_kernel,
        (shape(centroids.shape, centroids.dtype), shape(rows.shape, rows.dtype)),
        (rows,),
        "load_centroids",
        0,
        scratch=[pltpu.SemaphoreType.DMA(())],
        index=index,
        far=(centroids,),
    )


def first_score_kernel(index_ref, rows_ref, cent_ref, score_ref, top_ref, ordered):
    order_rows(index_ref, rows_ref, ordered)
    rows, top = ordered[...], None
    for chunk in range(cent_ref.shape[0] // CHUNK):
        top = score_chunk(rows, cent_ref, score_ref, chunk, top)
    top_ref[...] = top


def second_score_kernel(
    index_ref, score_ref, lane_top_ref, rows_ref, cent_ref, tile_ref, top_ref, total_ref, held, ordered
):
    first, second = block_starts(index_ref, 0), block_starts(index_ref, 1)
    row_top = jnp.max(lane_top_ref[...], axis=1, keepdims=True)
    order_rows(index_ref, rows_ref, ordered)
    rows, top, total = ordered[...], None, None
    for chunk in range(cent_ref.shape[0] // CHUNK):
        top = score_chunk(rows, cent_ref, held, chunk, top)
        total = exp_chunk(score_ref, tile_ref, first, chunk, row_top, total)
    store_stat(top_ref, first, to_lanes(lane_top_ref[...], jnp.max))
    store_stat(total_ref, first, to_lanes(total, jnp.sum))
    row_top = jnp.max(top, axis=1, keepdims=True)
    total = None
    for chunk in range(cent_ref.shape[0] // CHUNK):
        total = exp_chunk(held, tile_ref, second, chunk, row_top, total)
    store_stat(top_ref, second, to_lanes(top, jnp.max))
    store_stat(total_ref, second, to_lanes(total, jnp.sum))


def score_both(index, first_rows, second_rows, near):
    rows, features = first_rows.shape
    columns = near.shape[0]
    shape = jax.ShapeDtypeStruct
    flops = 2 * rows * columns * features
    scores, lane_top = call_kernel(
        first_score_kernel,
        (shape((rows, columns), F32), shape((rows, 128), F32)),
        (first_rows, near),
        "score_first",
        flops,
        scratch=[pltpu.VMEM(first_rows.shape, BF16)],
        index=index,
    )
    stats = shape((1, 2 * rows), F32)
    tile, top, total = call_kernel(
        second_score_kernel,
        (shape((2 * rows, columns), BF16), stats, stats),
        (scores, lane_top, second_rows, near),
        "score_second",
        flops,
        2 * rows * columns,
        [pltpu.VMEM((rows, columns), F32), pltpu.VMEM(first_rows.shape, BF16)],
        scoped=20,
        index=index,
    )
    return tile, top[0], total[0]


def down_rows(vector):
    groups = [
        jnp.transpose(jnp.broadcast_to(vector[:, g * 128 : (g + 1) * 128], (128, 128)))
        for g in range(vector.shape[1] // 128)
    ]
    return jnp.concatenate(groups, axis=0)


def half_rows(index_ref, part, half):
    return pl.ds(pl.multiple_of(((index_ref[0] & 1) ^ part) * half, half), half)


def positive_kernel(part, index_ref, tile_ref, cent_ref, pass_ref, out_ref, passed_ref):
    passed_ref[...] = pass_ref[...]
    rows = half_rows(index_ref, part, out_ref.shape[0])
    out_ref[...] = jnp.dot(tile_ref[rows, :], cent_ref[...], preferred_element_type=F32)


def negative_kernel(
    part, index_ref, tile_ref, cent_ref, pass_ref, column_ref, out_ref, passed_ref
):
    passed_ref[...] = pass_ref[...]
    rows = half_rows(index_ref, part, out_ref.shape[0])
    width = 256
    total = None
    for chunk in range(tile_ref.shape[1] // width):
        columns = slice(chunk * width, (chunk + 1) * width)
        weights = (tile_ref[rows, columns].astype(F32) * column_ref[:, columns]).astype(BF16)
        product = jnp.dot(weights, cent_ref[columns, :], preferred_element_type=F32)
        total = product if total is None else total + product
    out_ref[...] = total


def half_products(kernel, index, tile, centroids, passed, *vectors):
    rows, columns = tile.shape[0] // 2, tile.shape[1]
    features = centroids.shape[1]
    shape = jax.ShapeDtypeStruct
    products, passed = [], passed[None, :]
    for part in range(2):
        product, passed = call_kernel(
            functools.partial(kernel, part),
            (shape((rows, features), F32), shape(passed.shape, passed.dtype)),
            (tile, centroids, passed) + vectors,
            kernel.__name__,
            2 * rows * columns * features,
            index=index,
        )
        products.append(product)
    return products, passed[0]


def combine_kernel(part, index_ref, positive_ref, negative_ref, up_ref, down_ref, out_ref):
    y = index_ref[0] >> 3
    repeat = positive_ref.shape[1] // 128
    for m, start in enumerate(block_starts(index_ref, part)):
        up, down = [
            jnp.concatenate([down_rows(ref[:, pl.ds(start, 128)])] * repeat, axis=1)
            for ref in (up_ref, down_ref)
        ]
        source = pl.ds(pl.multiple_of((y ^ m) * 128, 128), 128)
        rows = positive_ref[source, :] * up - negative_ref[source, :] * down
        for k, place in enumerate(z_starts(index_ref)):
            target = pl.ds(pl.multiple_of(m * 128 + place, 32), 32)
            out_ref[target, :] = rows[k * 32 : (k + 1) * 32].astype(out_ref.dtype)


def combine(part, index, positive, negative, up, down, dtype):
    return call_kernel(
        functools.partial(combine_kernel, part),
        (jax.ShapeDtypeStruct(positive.shape, dtype),),
        (positive, negative, up[None, :], down[None, :]),
        "combine",
        3 * positive.size,
        index=index,
    )[0]


def swap(value, mask):
    size = lax.axis_size("cent")
    return lax.ppermute(value, "cent", [(i, i ^ mask) for i in range(size)])


def swap_three(values, masks):
    near, far, other = masks
    first, last = swap(values[0], near), swap(values[2], other)
    return [first, swap(values[1], far), last]


def sum_cent(value):
    value = value + swap(value, CORE)
    for masks in (ALONG_Y, ALONG_Z):
        value = value + sum(swap_three([value] * 3, masks))
    return value


def sum_batch(value):
    others = [
        lax.ppermute(value, "batch", [(i, i ^ mask) for i in range(4)]) for mask in (1, 3, 2)
    ]
    return value + sum(others)


def merge_softmax(top, total):
    pair = jnp.stack([top, total])
    for masks in ((CORE,), ALONG_Y, ALONG_Z):
        pairs = [pair] + (swap_three([pair] * 3, masks) if len(masks) == 3 else [swap(pair, CORE)])
        new_top = pairs[0][0]
        for other in pairs[1:]:
            new_top = jnp.maximum(new_top, other[0])
        new_total = sum([other[1] * jnp.exp(other[0] - new_top) for other in pairs])
        pair = jnp.stack([new_top, new_total])
    return pair[0], pair[1]


def scatter_stage(blocks, masks):
    arrived = swap_three([block.astype(BF16) for block in blocks[1:]], masks)
    return blocks[0] + sum([value.astype(F32) for value in arrived])


def per_device(queries, centroids, centroid_mass):
    where = lax.axis_index("cent").astype(jnp.int32).reshape(1)
    plane = jnp.concatenate([queries] + swap_three([queries] * 3, ALONG_Z))
    near, own_plane = load_near(where, centroids, plane)
    own_rows = jnp.concatenate([own_plane] + swap_three([plane] * 3, ALONG_Y))
    far_rows = swap(own_rows, CORE)
    tile, block_peak_max, block_total = score_both(where, own_rows, far_rows, near)
    positive, passed = half_products(positive_kernel, where, tile, near, block_peak_max)
    row_max, partition = merge_softmax(block_peak_max, block_total)
    block_peak_max = passed
    balance_factor = jnp.exp(block_peak_max - row_max)
    up = weights = balance_factor / partition
    for sweep in range(ITERS):
        column = jnp.dot(weights, tile, preferred_element_type=F32)
        column_scales = centroid_mass / sum_batch(column)
        row_local = jnp.dot(tile, column_scales, preferred_element_type=F32)
        row_sums = sum_cent(balance_factor * row_local)
        if sweep == ITERS - 1:
            small = (column_scales * 2.0**-6)[None, :]
            negative, balance_factor = half_products(
                negative_kernel, where, tile, near, balance_factor, small
            )
        weights = balance_factor / row_sums
    down = weights * 2.0**6

    far_sum = swap(combine(1, where, positive[1], negative[1], up, down, BF16), CORE)
    rows = combine(0, where, positive[0], negative[0], up, down, F32) + far_sum.astype(F32)
    plane_sum = scatter_stage(jnp.split(rows, 4), ALONG_Y)
    return scatter_stage(jnp.split(plane_sum, 4), ALONG_Z)


def solution(mesh):
    placed = (P(("batch", "cent"), None), P("cent", None), P("cent"))
    return jax.shard_map(
        per_device,
        mesh=mesh,
        in_specs=placed,
        out_specs=P(("batch", "cent"), None),
        check_vma=False,
    )
```

```python
import functools

import jax
import jax.numpy as jnp
from jax import lax
from jax.experimental import pallas as pl
from jax.experimental.pallas import tpu as pltpu
from jax.sharding import PartitionSpec as P

ITERS = 3
CORE = 1
ALONG_Z = (2, 4, 6)
ALONG_Y = (8, 16, 24)
LARGE = tuple(zip(ALONG_Y, ALONG_Z))
SMALL = tuple(zip(ALONG_Z, ALONG_Y))
F32 = jnp.float32
BF16 = jnp.bfloat16
VMEM = pl.BlockSpec(memory_space=pltpu.VMEM)
CHUNK = 512


def call_kernel(
    kernel, outs, args, name, flops, transcendentals=0, scratch=(), scoped=12, index=None, far=()
):
    moved = sum(a.size * a.dtype.itemsize for a in list(args) + list(outs) + list(far))
    args = [pltpu.with_memory_space_constraint(a, pltpu.VMEM) for a in args]
    specs = [VMEM] * len(args)
    args = [pltpu.with_memory_space_constraint(a, pltpu.HBM) for a in far] + args
    specs = [pl.BlockSpec(memory_space=pltpu.HBM)] * len(far) + specs
    if index is not None:
        args, specs = [index] + args, [pl.BlockSpec(memory_space=pltpu.SMEM)] + specs
    return pl.pallas_call(
        kernel,
        out_shape=tuple(pltpu.VMEM(o.shape, o.dtype) for o in outs),
        in_specs=specs,
        out_specs=(VMEM,) * len(outs),
        scratch_shapes=list(scratch),
        compiler_params=pltpu.CompilerParams(vmem_limit_bytes=scoped * 2**20),
        cost_estimate=pl.CostEstimate(
            flops=flops, bytes_accessed=moved, transcendentals=transcendentals
        ),
        name=name,
    )(*args)


def lane_groups(value, op, start):
    for group in range(value.shape[1] // 128):
        part = value[:, group * 128 : (group + 1) * 128]
        start = part if start is None else op(start, part)
    return start


def to_lanes(value, op):
    return op(jnp.transpose(value), axis=0, keepdims=True)


def z_starts(index_ref):
    z = (index_ref[0] >> 1) & 3
    return [pl.multiple_of((z ^ k) * 32, 32) for k in range(4)]


def order_rows(index_ref, part, rows_ref, ordered):
    of_first_core = (index_ref[0] & 1) == part
    starts = z_starts(index_ref)
    for m in range(4):
        for k in range(4):
            place = jnp.where(of_first_core, m * 128 + starts[k], k * 128 + starts[m])
            rows = rows_ref[m * 128 + k * 32 : m * 128 + (k + 1) * 32, :]
            ordered[pl.ds(pl.multiple_of(place, 32), 32), :] = rows


def score_chunk(rows, cent_ref, score_ref, chunk, top):
    columns = slice(chunk * CHUNK, (chunk + 1) * CHUNK)
    scores = lax.dot_general(
        rows, cent_ref[columns, :], (((1,), (1,)), ((), ())), preferred_element_type=F32
    )
    score_ref[:, columns] = scores
    return lane_groups(scores, jnp.maximum, top)


def block_starts(index_ref, part):
    core, y = index_ref[0] & 1, index_ref[0] >> 3
    return [pl.multiple_of((core ^ part) * 512 + (y ^ m) * 128, 128) for m in range(4)]


def exp_chunk(score_ref, tile_ref, starts, chunk, top, total):
    columns = slice(chunk * CHUNK, (chunk + 1) * CHUNK)
    shifted = jnp.exp(score_ref[:, columns] - top)
    rounded = shifted.astype(BF16)
    for m, start in enumerate(starts):
        tile_ref[pl.ds(start, 128), columns] = rounded[m * 128 : (m + 1) * 128]
    return lane_groups(shifted, jnp.add, total)


def store_stat(out_ref, starts, lanes):
    for m, start in enumerate(starts):
        out_ref[:, pl.ds(start, 128)] = lanes[:, m * 128 : (m + 1) * 128]


def load_kernel(index_ref, far_ref, rows_ref, near_ref, out_ref, arrived):
    copy = pltpu.make_async_copy(far_ref, near_ref, arrived)
    copy.start()
    out_ref[...] = rows_ref[...]
    copy.wait()


def load_near(index, centroids, rows):
    shape = jax.ShapeDtypeStruct
    return call_kernel(
        load_kernel,
        (shape(centroids.shape, centroids.dtype), shape(rows.shape, rows.dtype)),
        (rows,),
        "load_centroids",
        0,
        scratch=[pltpu.SemaphoreType.DMA(())],
        index=index,
        far=(centroids,),
    )


def first_score_kernel(index_ref, rows_ref, cent_ref, score_ref, top_ref, ordered):
    order_rows(index_ref, 0, rows_ref, ordered)
    rows, top = ordered[...], None
    for chunk in range(cent_ref.shape[0] // CHUNK):
        top = score_chunk(rows, cent_ref, score_ref, chunk, top)
    top_ref[...] = top


def second_score_kernel(
    index_ref, score_ref, lane_top_ref, rows_ref, cent_ref, tile_ref, top_ref, total_ref, held, ordered
):
    first, second = block_starts(index_ref, 0), block_starts(index_ref, 1)
    row_top = jnp.max(lane_top_ref[...], axis=1, keepdims=True)
    order_rows(index_ref, 1, rows_ref, ordered)
    rows, top, total = ordered[...], None, None
    for chunk in range(cent_ref.shape[0] // CHUNK):
        top = score_chunk(rows, cent_ref, held, chunk, top)
        total = exp_chunk(score_ref, tile_ref, first, chunk, row_top, total)
    store_stat(top_ref, first, to_lanes(lane_top_ref[...], jnp.max))
    store_stat(total_ref, first, to_lanes(total, jnp.sum))
    row_top = jnp.max(top, axis=1, keepdims=True)
    total = None
    for chunk in range(cent_ref.shape[0] // CHUNK):
        total = exp_chunk(held, tile_ref, second, chunk, row_top, total)
    store_stat(top_ref, second, to_lanes(top, jnp.max))
    store_stat(total_ref, second, to_lanes(total, jnp.sum))


def score_both(index, first_rows, second_rows, near):
    rows, features = first_rows.shape
    columns = near.shape[0]
    shape = jax.ShapeDtypeStruct
    flops = 2 * rows * columns * features
    scores, lane_top = call_kernel(
        first_score_kernel,
        (shape((rows, columns), F32), shape((rows, 128), F32)),
        (first_rows, near),
        "score_first",
        flops,
        scratch=[pltpu.VMEM(first_rows.shape, BF16)],
        index=index,
    )
    stats = shape((1, 2 * rows), F32)
    tile, top, total = call_kernel(
        second_score_kernel,
        (shape((2 * rows, columns), BF16), stats, stats),
        (scores, lane_top, second_rows, near),
        "score_second",
        flops,
        2 * rows * columns,
        [pltpu.VMEM((rows, columns), F32), pltpu.VMEM(first_rows.shape, BF16)],
        scoped=20,
        index=index,
    )
    return tile, top[0], total[0]


def down_rows(vector):
    groups = [
        jnp.transpose(jnp.broadcast_to(vector[:, g * 128 : (g + 1) * 128], (128, 128)))
        for g in range(vector.shape[1] // 128)
    ]
    return jnp.concatenate(groups, axis=0)


def half_rows(index_ref, part, half):
    return pl.ds(pl.multiple_of(((index_ref[0] & 1) ^ part) * half, half), half)


def positive_kernel(part, index_ref, tile_ref, cent_ref, pass_ref, out_ref, passed_ref):
    passed_ref[...] = pass_ref[...]
    rows = half_rows(index_ref, part, out_ref.shape[0])
    out_ref[...] = jnp.dot(tile_ref[rows, :], cent_ref[...], preferred_element_type=F32)


def negative_kernel(
    part, index_ref, tile_ref, cent_ref, pass_ref, column_ref, out_ref, passed_ref
):
    passed_ref[...] = pass_ref[...]
    rows = half_rows(index_ref, part, out_ref.shape[0])
    width = 256
    total = None
    for chunk in range(tile_ref.shape[1] // width):
        columns = slice(chunk * width, (chunk + 1) * width)
        weights = (tile_ref[rows, columns].astype(F32) * column_ref[:, columns]).astype(BF16)
        product = jnp.dot(weights, cent_ref[columns, :], preferred_element_type=F32)
        total = product if total is None else total + product
    out_ref[...] = total


def half_products(kernel, index, tile, centroids, passed, *vectors):
    rows, columns = tile.shape[0] // 2, tile.shape[1]
    features = centroids.shape[1]
    shape = jax.ShapeDtypeStruct
    products, passed = [], passed[None, :]
    for part in range(2):
        product, passed = call_kernel(
            functools.partial(kernel, part),
            (shape((rows, features), F32), shape(passed.shape, passed.dtype)),
            (tile, centroids, passed) + vectors,
            kernel.__name__,
            2 * rows * columns * features,
            index=index,
        )
        products.append(product)
    return products, passed[0]


def combine_kernel(part, index_ref, positive_ref, negative_ref, up_ref, down_ref, out_ref):
    y = index_ref[0] >> 3
    for_first_core = (index_ref[0] & 1) == part
    repeat = positive_ref.shape[1] // 128
    for m, start in enumerate(block_starts(index_ref, part)):
        up, down = [
            jnp.concatenate([down_rows(ref[:, pl.ds(start, 128)])] * repeat, axis=1)
            for ref in (up_ref, down_ref)
        ]
        source = pl.ds(pl.multiple_of((y ^ m) * 128, 128), 128)
        rows = positive_ref[source, :] * up - negative_ref[source, :] * down
        for k, place in enumerate(z_starts(index_ref)):
            target = jnp.where(for_first_core, m * 128 + place, place * 4 + m * 32)
            target = pl.ds(pl.multiple_of(target, 32), 32)
            out_ref[target, :] = rows[k * 32 : (k + 1) * 32].astype(out_ref.dtype)


def combine(part, index, positive, negative, up, down, dtype):
    return call_kernel(
        functools.partial(combine_kernel, part),
        (jax.ShapeDtypeStruct(positive.shape, dtype),),
        (positive, negative, up[None, :], down[None, :]),
        "combine",
        3 * positive.size,
        index=index,
    )[0]


def swap(value, mask):
    size = lax.axis_size("cent")
    masks = mask if isinstance(mask, tuple) else (mask, mask)
    return lax.ppermute(value, "cent", [(i, i ^ masks[i & 1]) for i in range(size)])


def swap_three(values, masks):
    near, far, other = masks
    first, last = swap(values[0], near), swap(values[2], other)
    return [first, swap(values[1], far), last]


def sum_cent(value):
    value = value + swap(value, CORE)
    for masks in (ALONG_Y, ALONG_Z):
        value = value + sum(swap_three([value] * 3, masks))
    return value


def sum_batch(value):
    others = [
        lax.ppermute(value, "batch", [(i, i ^ mask) for i in range(4)]) for mask in (1, 3, 2)
    ]
    return value + sum(others)


def merge_softmax(top, total):
    pair = jnp.stack([top, total])
    for masks in ((CORE,), ALONG_Y, ALONG_Z):
        pairs = [pair] + (swap_three([pair] * 3, masks) if len(masks) == 3 else [swap(pair, CORE)])
        new_top = pairs[0][0]
        for other in pairs[1:]:
            new_top = jnp.maximum(new_top, other[0])
        new_total = sum([other[1] * jnp.exp(other[0] - new_top) for other in pairs])
        pair = jnp.stack([new_top, new_total])
    return pair[0], pair[1]


def scatter_stage(blocks, masks):
    arrived = swap_three([block.astype(BF16) for block in blocks[1:]], masks)
    return blocks[0] + sum([value.astype(F32) for value in arrived])


def per_device(queries, centroids, centroid_mass):
    where = lax.axis_index("cent").astype(jnp.int32).reshape(1)
    plane = jnp.concatenate([queries] + swap_three([queries] * 3, SMALL))
    near, own_plane = load_near(where, centroids, plane)
    own_rows = jnp.concatenate([own_plane] + swap_three([plane] * 3, LARGE))
    far_rows = swap(own_rows, CORE)
    tile, block_peak_max, block_total = score_both(where, own_rows, far_rows, near)
    positive, passed = half_products(positive_kernel, where, tile, near, block_peak_max)
    row_max, partition = merge_softmax(block_peak_max, block_total)
    block_peak_max = passed
    balance_factor = jnp.exp(block_peak_max - row_max)
    up = weights = balance_factor / partition
    for sweep in range(ITERS):
        column = jnp.dot(weights, tile, preferred_element_type=F32)
        column_scales = centroid_mass / sum_batch(column)
        row_local = jnp.dot(tile, column_scales, preferred_element_type=F32)
        row_sums = sum_cent(balance_factor * row_local)
        if sweep == ITERS - 1:
            small = (column_scales * 2.0**-6)[None, :]
            negative, balance_factor = half_products(
                negative_kernel, where, tile, near, balance_factor, small
            )
        weights = balance_factor / row_sums
    down = weights * 2.0**6

    far_sum = swap(combine(1, where, positive[1], negative[1], up, down, BF16), CORE)
    rows = combine(0, where, positive[0], negative[0], up, down, F32) + far_sum.astype(F32)
    plane_sum = scatter_stage(jnp.split(rows, 4), LARGE)
    return scatter_stage(jnp.split(plane_sum, 4), SMALL)


def solution(mesh):
    placed = (P(("batch", "cent"), None), P("cent", None), P("cent"))
    return jax.shard_map(
        per_device,
        mesh=mesh,
        in_specs=placed,
        out_specs=P(("batch", "cent"), None),
        check_vma=False,
    )
```

```python
import functools

import jax
import jax.numpy as jnp
from jax import lax
from jax.experimental import pallas as pl
from jax.experimental.pallas import tpu as pltpu
from jax.sharding import PartitionSpec as P

ITERS = 3
CORE = 1
ALONG_Z = (2, 4, 6)
ALONG_Y = (8, 16, 24)
LARGE = tuple(zip(ALONG_Y, ALONG_Z))
SMALL = tuple(zip(ALONG_Z, ALONG_Y))
F32 = jnp.float32
BF16 = jnp.bfloat16
VMEM = pl.BlockSpec(memory_space=pltpu.VMEM)
CHUNK = 512


def call_kernel(
    kernel, outs, args, name, flops, transcendentals=0, scratch=(), scoped=12, index=None, far=()
):
    moved = sum(a.size * a.dtype.itemsize for a in list(args) + list(outs) + list(far))
    args = [pltpu.with_memory_space_constraint(a, pltpu.VMEM) for a in args]
    specs = [VMEM] * len(args)
    args = [pltpu.with_memory_space_constraint(a, pltpu.HBM) for a in far] + args
    specs = [pl.BlockSpec(memory_space=pltpu.HBM)] * len(far) + specs
    if index is not None:
        args, specs = [index] + args, [pl.BlockSpec(memory_space=pltpu.SMEM)] + specs
    return pl.pallas_call(
        kernel,
        out_shape=tuple(pltpu.VMEM(o.shape, o.dtype) for o in outs),
        in_specs=specs,
        out_specs=(VMEM,) * len(outs),
        scratch_shapes=list(scratch),
        compiler_params=pltpu.CompilerParams(vmem_limit_bytes=scoped * 2**20),
        cost_estimate=pl.CostEstimate(
            flops=flops, bytes_accessed=moved, transcendentals=transcendentals
        ),
        name=name,
    )(*args)


def lane_groups(value, op, start):
    for group in range(value.shape[1] // 128):
        part = value[:, group * 128 : (group + 1) * 128]
        start = part if start is None else op(start, part)
    return start


def to_lanes(value, op):
    return op(jnp.transpose(value), axis=0, keepdims=True)


def z_starts(index_ref):
    z = (index_ref[0] >> 1) & 3
    return [pl.multiple_of((z ^ k) * 32, 32) for k in range(4)]


def order_rows(index_ref, part, rows_ref, ordered):
    of_first_core = (index_ref[0] & 1) == part
    starts = z_starts(index_ref)
    for m in range(4):
        for k in range(4):
            place = jnp.where(of_first_core, m * 128 + starts[k], k * 128 + starts[m])
            rows = rows_ref[m * 128 + k * 32 : m * 128 + (k + 1) * 32, :]
            ordered[pl.ds(pl.multiple_of(place, 32), 32), :] = rows


def score_chunk(rows, cent_ref, score_ref, chunk, top):
    columns = slice(chunk * CHUNK, (chunk + 1) * CHUNK)
    scores = lax.dot_general(
        rows, cent_ref[columns, :], (((1,), (1,)), ((), ())), preferred_element_type=F32
    )
    score_ref[:, columns] = scores
    return lane_groups(scores, jnp.maximum, top)


def block_starts(index_ref, part):
    core, y = index_ref[0] & 1, index_ref[0] >> 3
    return [pl.multiple_of((core ^ part) * 512 + (y ^ m) * 128, 128) for m in range(4)]


def exp_chunk(score_ref, tile_ref, starts, chunk, top, total):
    columns = slice(chunk * CHUNK, (chunk + 1) * CHUNK)
    shifted = jnp.exp(score_ref[:, columns] - top)
    rounded = shifted.astype(BF16)
    for m, start in enumerate(starts):
        tile_ref[pl.ds(start, 128), columns] = rounded[m * 128 : (m + 1) * 128]
    return lane_groups(shifted, jnp.add, total)


def store_stat(out_ref, starts, lanes):
    for m, start in enumerate(starts):
        out_ref[:, pl.ds(start, 128)] = lanes[:, m * 128 : (m + 1) * 128]


def load_kernel(index_ref, far_ref, rows_ref, near_ref, out_ref, arrived):
    copy = pltpu.make_async_copy(far_ref, near_ref, arrived)
    copy.start()
    out_ref[...] = rows_ref[...]
    copy.wait()


def load_near(index, centroids, rows):
    shape = jax.ShapeDtypeStruct
    return call_kernel(
        load_kernel,
        (shape(centroids.shape, centroids.dtype), shape(rows.shape, rows.dtype)),
        (rows,),
        "load_centroids",
        0,
        scratch=[pltpu.SemaphoreType.DMA(())],
        index=index,
        far=(centroids,),
    )


def first_score_kernel(index_ref, rows_ref, cent_ref, score_ref, top_ref, ordered):
    order_rows(index_ref, 0, rows_ref, ordered)
    rows, top = ordered[...], None
    for chunk in range(cent_ref.shape[0] // CHUNK):
        top = score_chunk(rows, cent_ref, score_ref, chunk, top)
    top_ref[...] = top


def second_score_kernel(
    index_ref, score_ref, lane_top_ref, rows_ref, cent_ref, tile_ref, top_ref, total_ref, held, ordered
):
    first, second = block_starts(index_ref, 0), block_starts(index_ref, 1)
    row_top = jnp.max(lane_top_ref[...], axis=1, keepdims=True)
    order_rows(index_ref, 1, rows_ref, ordered)
    rows, top, total = ordered[...], None, None
    for chunk in range(cent_ref.shape[0] // CHUNK):
        top = score_chunk(rows, cent_ref, held, chunk, top)
        total = exp_chunk(score_ref, tile_ref, first, chunk, row_top, total)
    store_stat(top_ref, first, to_lanes(lane_top_ref[...], jnp.max))
    store_stat(total_ref, first, to_lanes(total, jnp.sum))
    row_top = jnp.max(top, axis=1, keepdims=True)
    total = None
    for chunk in range(cent_ref.shape[0] // CHUNK):
        total = exp_chunk(held, tile_ref, second, chunk, row_top, total)
    store_stat(top_ref, second, to_lanes(top, jnp.max))
    store_stat(total_ref, second, to_lanes(total, jnp.sum))


def score_both(index, first_rows, second_rows, near):
    rows, features = first_rows.shape
    columns = near.shape[0]
    shape = jax.ShapeDtypeStruct
    flops = 2 * rows * columns * features
    scores, lane_top = call_kernel(
        first_score_kernel,
        (shape((rows, columns), F32), shape((rows, 128), F32)),
        (first_rows, near),
        "score_first",
        flops,
        scratch=[pltpu.VMEM(first_rows.shape, BF16)],
        index=index,
    )
    stats = shape((1, 2 * rows), F32)
    tile, top, total = call_kernel(
        second_score_kernel,
        (shape((2 * rows, columns), BF16), stats, stats),
        (scores, lane_top, second_rows, near),
        "score_second",
        flops,
        2 * rows * columns,
        [pltpu.VMEM((rows, columns), F32), pltpu.VMEM(first_rows.shape, BF16)],
        scoped=20,
        index=index,
    )
    return tile, top[0], total[0]


def down_rows(vector):
    groups = [
        jnp.transpose(jnp.broadcast_to(vector[:, g * 128 : (g + 1) * 128], (128, 128)))
        for g in range(vector.shape[1] // 128)
    ]
    return jnp.concatenate(groups, axis=0)


def split_exact(vector):
    high = vector.astype(BF16)
    rest = vector - high.astype(F32)
    middle = rest.astype(BF16)
    low = (rest - middle.astype(F32)).astype(BF16)
    return jnp.concatenate([high, middle, low], axis=0)


def row_sum_kernel(tile_ref, column_ref, out_ref):
    half = tile_ref.shape[0] // 2
    parts = lax.dot_general(
        split_exact(column_ref[...]),
        tile_ref[:half, :],
        (((1,), (1,)), ((), ())),
        preferred_element_type=F32,
    )
    total = None
    for start in range(0, tile_ref.shape[1], 128):
        columns = slice(start, start + 128)
        part = tile_ref[half:, columns].astype(F32) * column_ref[:, columns]
        total = part if total is None else total + part
    out_ref[:, :half] = jnp.sum(parts, axis=0, keepdims=True)
    out_ref[:, half:] = to_lanes(total, jnp.sum)


def row_sums_of(tile, column_scales):
    return call_kernel(
        row_sum_kernel,
        (jax.ShapeDtypeStruct((1, tile.shape[0]), F32),),
        (tile, column_scales[None, :]),
        "row_sums",
        2 * tile.size,
    )[0][0]


def half_rows(index_ref, part, half):
    return pl.ds(pl.multiple_of(((index_ref[0] & 1) ^ part) * half, half), half)


def positive_kernel(part, index_ref, tile_ref, cent_ref, pass_ref, out_ref, passed_ref):
    passed_ref[...] = pass_ref[...]
    rows = half_rows(index_ref, part, out_ref.shape[0])
    out_ref[...] = jnp.dot(tile_ref[rows, :], cent_ref[...], preferred_element_type=F32)


def negative_kernel(
    part, index_ref, tile_ref, cent_ref, pass_ref, column_ref, out_ref, passed_ref
):
    passed_ref[...] = pass_ref[...]
    rows = half_rows(index_ref, part, out_ref.shape[0])
    width = 256
    total = None
    for chunk in range(tile_ref.shape[1] // width):
        columns = slice(chunk * width, (chunk + 1) * width)
        weights = (tile_ref[rows, columns].astype(F32) * column_ref[:, columns]).astype(BF16)
        product = jnp.dot(weights, cent_ref[columns, :], preferred_element_type=F32)
        total = product if total is None else total + product
    out_ref[...] = total


def half_products(kernel, index, tile, centroids, passed, *vectors):
    rows, columns = tile.shape[0] // 2, tile.shape[1]
    features = centroids.shape[1]
    shape = jax.ShapeDtypeStruct
    products, passed = [], passed[None, :]
    for part in range(2):
        product, passed = call_kernel(
            functools.partial(kernel, part),
            (shape((rows, features), F32), shape(passed.shape, passed.dtype)),
            (tile, centroids, passed) + vectors,
            kernel.__name__,
            2 * rows * columns * features,
            index=index,
        )
        products.append(product)
    return products, passed[0]


def combine_kernel(part, index_ref, positive_ref, negative_ref, up_ref, down_ref, out_ref):
    y = index_ref[0] >> 3
    for_first_core = (index_ref[0] & 1) == part
    repeat = positive_ref.shape[1] // 128
    for m, start in enumerate(block_starts(index_ref, part)):
        up, down = [
            jnp.concatenate([down_rows(ref[:, pl.ds(start, 128)])] * repeat, axis=1)
            for ref in (up_ref, down_ref)
        ]
        source = pl.ds(pl.multiple_of((y ^ m) * 128, 128), 128)
        rows = positive_ref[source, :] * up - negative_ref[source, :] * down
        for k, place in enumerate(z_starts(index_ref)):
            target = jnp.where(for_first_core, m * 128 + place, place * 4 + m * 32)
            target = pl.ds(pl.multiple_of(target, 32), 32)
            out_ref[target, :] = rows[k * 32 : (k + 1) * 32].astype(out_ref.dtype)


def combine(part, index, positive, negative, up, down, dtype):
    return call_kernel(
        functools.partial(combine_kernel, part),
        (jax.ShapeDtypeStruct(positive.shape, dtype),),
        (positive, negative, up[None, :], down[None, :]),
        "combine",
        3 * positive.size,
        index=index,
    )[0]


def swap(value, mask):
    size = lax.axis_size("cent")
    masks = mask if isinstance(mask, tuple) else (mask, mask)
    return lax.ppermute(value, "cent", [(i, i ^ masks[i & 1]) for i in range(size)])


def swap_three(values, masks):
    near, far, other = masks
    first, last = swap(values[0], near), swap(values[2], other)
    return [first, swap(values[1], far), last]


def sum_cent(value):
    value = value + swap(value, CORE)
    for masks in (LARGE, SMALL):
        value = value + sum(swap_three([value] * 3, masks))
    return value


def sum_batch(value):
    others = [
        lax.ppermute(value, "batch", [(i, i ^ mask) for i in range(4)]) for mask in (1, 3, 2)
    ]
    return value + sum(others)


def merge_softmax(top, total):
    pair = jnp.stack([top, total])
    for masks in ((CORE,), LARGE, SMALL):
        pairs = [pair] + (swap_three([pair] * 3, masks) if len(masks) == 3 else [swap(pair, CORE)])
        new_top = pairs[0][0]
        for other in pairs[1:]:
            new_top = jnp.maximum(new_top, other[0])
        new_total = sum([other[1] * jnp.exp(other[0] - new_top) for other in pairs])
        pair = jnp.stack([new_top, new_total])
    return pair[0], pair[1]


def scatter_stage(blocks, masks):
    arrived = swap_three([block.astype(BF16) for block in blocks[1:]], masks)
    return blocks[0] + sum([value.astype(F32) for value in arrived])


def per_device(queries, centroids, centroid_mass):
    where = lax.axis_index("cent").astype(jnp.int32).reshape(1)
    plane = jnp.concatenate([queries] + swap_three([queries] * 3, SMALL))
    near, own_plane = load_near(where, centroids, plane)
    own_rows = jnp.concatenate([own_plane] + swap_three([plane] * 3, LARGE))
    far_rows = swap(own_rows, CORE)
    tile, block_peak_max, block_total = score_both(where, own_rows, far_rows, near)
    positive, passed = half_products(positive_kernel, where, tile, near, block_peak_max)
    row_max, partition = merge_softmax(block_peak_max, block_total)
    block_peak_max = passed
    balance_factor = jnp.exp(block_peak_max - row_max)
    up = weights = balance_factor / partition
    for sweep in range(ITERS):
        column = jnp.dot(weights, tile, preferred_element_type=F32)
        column_scales = centroid_mass / sum_batch(column)
        row_local = row_sums_of(tile, column_scales)
        row_sums = sum_cent(balance_factor * row_local)
        if sweep == ITERS - 1:
            small = (column_scales * 2.0**-6)[None, :]
            negative, balance_factor = half_products(
                negative_kernel, where, tile, near, balance_factor, small
            )
        weights = balance_factor / row_sums
    down = weights * 2.0**6

    far_sum = swap(combine(1, where, positive[1], negative[1], up, down, BF16), CORE)
    rows = combine(0, where, positive[0], negative[0], up, down, F32) + far_sum.astype(F32)
    plane_sum = scatter_stage(jnp.split(rows, 4), LARGE)
    return scatter_stage(jnp.split(plane_sum, 4), SMALL)


def solution(mesh):
    placed = (P(("batch", "cent"), None), P("cent", None), P("cent"))
    return jax.shard_map(
        per_device,
        mesh=mesh,
        in_specs=placed,
        out_specs=P(("batch", "cent"), None),
        check_vma=False,
    )
```

```python
import functools

import jax
import jax.numpy as jnp
from jax import lax
from jax.experimental import pallas as pl
from jax.experimental.pallas import tpu as pltpu
from jax.sharding import PartitionSpec as P

ITERS = 3
CORE = 1
ALONG_Z = (2, 4, 6)
ALONG_Y = (8, 16, 24)
LARGE = tuple(zip(ALONG_Y, ALONG_Z))
SMALL = tuple(zip(ALONG_Z, ALONG_Y))
F32 = jnp.float32
BF16 = jnp.bfloat16
VMEM = pl.BlockSpec(memory_space=pltpu.VMEM)
CHUNK = 512


def call_kernel(
    kernel, outs, args, name, flops, transcendentals=0, scratch=(), scoped=12, index=None, far=()
):
    moved = sum(a.size * a.dtype.itemsize for a in list(args) + list(outs) + list(far))
    args = [pltpu.with_memory_space_constraint(a, pltpu.VMEM) for a in args]
    specs = [VMEM] * len(args)
    args = [pltpu.with_memory_space_constraint(a, pltpu.HBM) for a in far] + args
    specs = [pl.BlockSpec(memory_space=pltpu.HBM)] * len(far) + specs
    if index is not None:
        args, specs = [index] + args, [pl.BlockSpec(memory_space=pltpu.SMEM)] + specs
    return pl.pallas_call(
        kernel,
        out_shape=tuple(pltpu.VMEM(o.shape, o.dtype) for o in outs),
        in_specs=specs,
        out_specs=(VMEM,) * len(outs),
        scratch_shapes=list(scratch),
        compiler_params=pltpu.CompilerParams(vmem_limit_bytes=scoped * 2**20),
        cost_estimate=pl.CostEstimate(
            flops=flops, bytes_accessed=moved, transcendentals=transcendentals
        ),
        name=name,
    )(*args)


def lane_groups(value, op, start):
    for group in range(value.shape[1] // 128):
        part = value[:, group * 128 : (group + 1) * 128]
        start = part if start is None else op(start, part)
    return start


def to_lanes(value, op):
    return op(jnp.transpose(value), axis=0, keepdims=True)


def z_starts(index_ref):
    z = (index_ref[0] >> 1) & 3
    return [pl.multiple_of((z ^ k) * 32, 32) for k in range(4)]


def order_rows(index_ref, part, rows_ref, ordered):
    of_first_core = (index_ref[0] & 1) == part
    starts = z_starts(index_ref)
    for m in range(4):
        for k in range(4):
            place = jnp.where(of_first_core, m * 128 + starts[k], k * 128 + starts[m])
            rows = rows_ref[m * 128 + k * 32 : m * 128 + (k + 1) * 32, :]
            ordered[pl.ds(pl.multiple_of(place, 32), 32), :] = rows


def score_chunk(rows, cent_ref, score_ref, chunk, top):
    columns = slice(chunk * CHUNK, (chunk + 1) * CHUNK)
    scores = lax.dot_general(
        rows, cent_ref[columns, :], (((1,), (1,)), ((), ())), preferred_element_type=F32
    )
    score_ref[:, columns] = scores
    return lane_groups(scores, jnp.maximum, top)


def block_starts(index_ref, part):
    core, y = index_ref[0] & 1, index_ref[0] >> 3
    return [pl.multiple_of((core ^ part) * 512 + (y ^ m) * 128, 128) for m in range(4)]


def exp_chunk(score_ref, tile_ref, starts, chunk, top, total):
    columns = slice(chunk * CHUNK, (chunk + 1) * CHUNK)
    shifted = jnp.exp(score_ref[:, columns] - top)
    rounded = shifted.astype(BF16)
    for m, start in enumerate(starts):
        tile_ref[pl.ds(start, 128), columns] = rounded[m * 128 : (m + 1) * 128]
    return lane_groups(shifted, jnp.add, total)


def store_stat(out_ref, starts, lanes):
    for m, start in enumerate(starts):
        out_ref[:, pl.ds(start, 128)] = lanes[:, m * 128 : (m + 1) * 128]


def load_kernel(index_ref, far_ref, rows_ref, near_ref, out_ref, arrived):
    copy = pltpu.make_async_copy(far_ref, near_ref, arrived)
    copy.start()
    out_ref[...] = rows_ref[...]
    copy.wait()


def load_near(index, centroids, rows):
    shape = jax.ShapeDtypeStruct
    return call_kernel(
        load_kernel,
        (shape(centroids.shape, centroids.dtype), shape(rows.shape, rows.dtype)),
        (rows,),
        "load_centroids",
        0,
        scratch=[pltpu.SemaphoreType.DMA(())],
        index=index,
        far=(centroids,),
    )


def first_score_kernel(index_ref, rows_ref, cent_ref, score_ref, top_ref, ordered):
    order_rows(index_ref, 0, rows_ref, ordered)
    rows, top = ordered[...], None
    for chunk in range(cent_ref.shape[0] // CHUNK):
        top = score_chunk(rows, cent_ref, score_ref, chunk, top)
    top_ref[...] = top


def second_score_kernel(
    index_ref, score_ref, lane_top_ref, rows_ref, cent_ref, tile_ref, top_ref, total_ref, held, ordered
):
    first, second = block_starts(index_ref, 0), block_starts(index_ref, 1)
    row_top = jnp.max(lane_top_ref[...], axis=1, keepdims=True)
    order_rows(index_ref, 1, rows_ref, ordered)
    rows, top, total = ordered[...], None, None
    for chunk in range(cent_ref.shape[0] // CHUNK):
        top = score_chunk(rows, cent_ref, held, chunk, top)
        total = exp_chunk(score_ref, tile_ref, first, chunk, row_top, total)
    store_stat(top_ref, first, to_lanes(lane_top_ref[...], jnp.max))
    store_stat(total_ref, first, to_lanes(total, jnp.sum))
    row_top = jnp.max(top, axis=1, keepdims=True)
    total = None
    for chunk in range(cent_ref.shape[0] // CHUNK):
        total = exp_chunk(held, tile_ref, second, chunk, row_top, total)
    store_stat(top_ref, second, to_lanes(top, jnp.max))
    store_stat(total_ref, second, to_lanes(total, jnp.sum))


def score_both(index, first_rows, second_rows, near):
    rows, features = first_rows.shape
    columns = near.shape[0]
    shape = jax.ShapeDtypeStruct
    flops = 2 * rows * columns * features
    scores, lane_top = call_kernel(
        first_score_kernel,
        (shape((rows, columns), F32), shape((rows, 128), F32)),
        (first_rows, near),
        "score_first",
        flops,
        scratch=[pltpu.VMEM(first_rows.shape, BF16)],
        index=index,
    )
    stats = shape((1, 2 * rows), F32)
    tile, top, total = call_kernel(
        second_score_kernel,
        (shape((2 * rows, columns), BF16), stats, stats),
        (scores, lane_top, second_rows, near),
        "score_second",
        flops,
        2 * rows * columns,
        [pltpu.VMEM((rows, columns), F32), pltpu.VMEM(first_rows.shape, BF16)],
        scoped=20,
        index=index,
    )
    return tile, top[0], total[0]


def down_rows(vector):
    groups = [
        jnp.transpose(jnp.broadcast_to(vector[:, g * 128 : (g + 1) * 128], (128, 128)))
        for g in range(vector.shape[1] // 128)
    ]
    return jnp.concatenate(groups, axis=0)


def row_sum_kernel(tile_ref, column_ref, out_ref):
    for block in range(tile_ref.shape[0] // 128):
        rows = slice(block * 128, (block + 1) * 128)
        total = None
        for start in range(0, tile_ref.shape[1], 128):
            columns = slice(start, start + 128)
            part = tile_ref[rows, columns].astype(F32) * column_ref[:, columns]
            total = part if total is None else total + part
        out_ref[:, rows] = to_lanes(total, jnp.sum)


def row_sums_of(tile, column_scales):
    return call_kernel(
        row_sum_kernel,
        (jax.ShapeDtypeStruct((1, tile.shape[0]), F32),),
        (tile, column_scales[None, :]),
        "row_sums",
        2 * tile.size,
    )[0][0]


def half_rows(index_ref, part, half):
    return pl.ds(pl.multiple_of(((index_ref[0] & 1) ^ part) * half, half), half)


def positive_kernel(part, index_ref, tile_ref, cent_ref, pass_ref, out_ref, passed_ref):
    passed_ref[...] = pass_ref[...]
    rows = half_rows(index_ref, part, out_ref.shape[0])
    out_ref[...] = jnp.dot(tile_ref[rows, :], cent_ref[...], preferred_element_type=F32)


def negative_kernel(
    part, index_ref, tile_ref, cent_ref, pass_ref, column_ref, out_ref, passed_ref
):
    passed_ref[...] = pass_ref[...]
    rows = half_rows(index_ref, part, out_ref.shape[0])
    width = 256
    total = None
    for chunk in range(tile_ref.shape[1] // width):
        columns = slice(chunk * width, (chunk + 1) * width)
        weights = (tile_ref[rows, columns].astype(F32) * column_ref[:, columns]).astype(BF16)
        product = jnp.dot(weights, cent_ref[columns, :], preferred_element_type=F32)
        total = product if total is None else total + product
    out_ref[...] = total


def half_products(kernel, index, tile, centroids, passed, *vectors):
    rows, columns = tile.shape[0] // 2, tile.shape[1]
    features = centroids.shape[1]
    shape = jax.ShapeDtypeStruct
    products, passed = [], passed[None, :]
    for part in range(2):
        product, passed = call_kernel(
            functools.partial(kernel, part),
            (shape((rows, features), F32), shape(passed.shape, passed.dtype)),
            (tile, centroids, passed) + vectors,
            kernel.__name__,
            2 * rows * columns * features,
            index=index,
        )
        products.append(product)
    return products, passed[0]


def combine_kernel(part, index_ref, positive_ref, negative_ref, up_ref, down_ref, out_ref):
    y = index_ref[0] >> 3
    for_first_core = (index_ref[0] & 1) == part
    repeat = positive_ref.shape[1] // 128
    for m, start in enumerate(block_starts(index_ref, part)):
        up, down = [
            jnp.concatenate([down_rows(ref[:, pl.ds(start, 128)])] * repeat, axis=1)
            for ref in (up_ref, down_ref)
        ]
        source = pl.ds(pl.multiple_of((y ^ m) * 128, 128), 128)
        rows = positive_ref[source, :] * up - negative_ref[source, :] * down
        for k, place in enumerate(z_starts(index_ref)):
            target = jnp.where(for_first_core, m * 128 + place, place * 4 + m * 32)
            target = pl.ds(pl.multiple_of(target, 32), 32)
            out_ref[target, :] = rows[k * 32 : (k + 1) * 32].astype(out_ref.dtype)


def combine(part, index, positive, negative, up, down, dtype):
    return call_kernel(
        functools.partial(combine_kernel, part),
        (jax.ShapeDtypeStruct(positive.shape, dtype),),
        (positive, negative, up[None, :], down[None, :]),
        "combine",
        3 * positive.size,
        index=index,
    )[0]


def swap(value, mask):
    size = lax.axis_size("cent")
    masks = mask if isinstance(mask, tuple) else (mask, mask)
    return lax.ppermute(value, "cent", [(i, i ^ masks[i & 1]) for i in range(size)])


def swap_three(values, masks):
    near, far, other = masks
    first, last = swap(values[0], near), swap(values[2], other)
    return [first, swap(values[1], far), last]


def sum_cent(value):
    value = value + swap(value, CORE)
    for masks in (LARGE, SMALL):
        value = value + sum(swap_three([value] * 3, masks))
    return value


def sum_batch(value):
    others = [
        lax.ppermute(value, "batch", [(i, i ^ mask) for i in range(4)]) for mask in (1, 3, 2)
    ]
    return value + sum(others)


def merge_softmax(top, total):
    pair = jnp.stack([top, total])
    for masks in ((CORE,), LARGE, SMALL):
        pairs = [pair] + (swap_three([pair] * 3, masks) if len(masks) == 3 else [swap(pair, CORE)])
        new_top = pairs[0][0]
        for other in pairs[1:]:
            new_top = jnp.maximum(new_top, other[0])
        new_total = sum([other[1] * jnp.exp(other[0] - new_top) for other in pairs])
        pair = jnp.stack([new_top, new_total])
    return pair[0], pair[1]


def scatter_stage(blocks, masks):
    arrived = swap_three([block.astype(BF16) for block in blocks[1:]], masks)
    return blocks[0] + sum([value.astype(F32) for value in arrived])


def per_device(queries, centroids, centroid_mass):
    where = lax.axis_index("cent").astype(jnp.int32).reshape(1)
    plane = jnp.concatenate([queries] + swap_three([queries] * 3, SMALL))
    near, own_plane = load_near(where, centroids, plane)
    own_rows = jnp.concatenate([own_plane] + swap_three([plane] * 3, LARGE))
    far_rows = swap(own_rows, CORE)
    tile, block_peak_max, block_total = score_both(where, own_rows, far_rows, near)
    positive, passed = half_products(positive_kernel, where, tile, near, block_peak_max)
    row_max, partition = merge_softmax(block_peak_max, block_total)
    block_peak_max = passed
    balance_factor = jnp.exp(block_peak_max - row_max)
    up = weights = balance_factor / partition
    for sweep in range(ITERS):
        column = jnp.dot(weights, tile, preferred_element_type=F32)
        column_scales = centroid_mass / sum_batch(column)
        row_local = row_sums_of(tile, column_scales)
        row_sums = sum_cent(balance_factor * row_local)
        if sweep == ITERS - 1:
            small = (column_scales * 2.0**-6)[None, :]
            negative, balance_factor = half_products(
                negative_kernel, where, tile, near, balance_factor, small
            )
        weights = balance_factor / row_sums
    down = weights * 2.0**6

    far_sum = swap(combine(1, where, positive[1], negative[1], up, down, BF16), CORE)
    rows = combine(0, where, positive[0], negative[0], up, down, F32) + far_sum.astype(F32)
    plane_sum = scatter_stage(jnp.split(rows, 4), LARGE)
    return scatter_stage(jnp.split(plane_sum, 4), SMALL)


def solution(mesh):
    placed = (P(("batch", "cent"), None), P("cent", None), P("cent"))
    return jax.shard_map(
        per_device,
        mesh=mesh,
        in_specs=placed,
        out_specs=P(("batch", "cent"), None),
        check_vma=False,
    )
```
